32 devices in a mesh: patch: 8 (over z, x), tile: 4 (over y, core).
Axes of the slice: x: 2, y: 2, z: 4, core: 2. Of those that a mesh axis runs over, the one named last changes fastest.
Arguments:
- latents: float32 [1088, 128], P('patch')
- timestamps: int32 [1088], P('patch'), may hold values from 0 to 56, as said below
- cell_map: int32 [1024], replicated, may hold values from 0 to 1023, as said below
- w_video: bfloat16 [128, 3072], replicated, may hold values from -0.5 to 0.5
- w_audio: bfloat16 [128, 3072], replicated, may hold values from -0.5 to 0.5
- mod_scale: float32 [2, 3072], replicated, may hold values from -3 to 3
- mod_shift: float32 [2, 3072], replicated, may hold values from -3 to 3
- w_query: bfloat16 [3072, 3072], P(None, 'tile')
- w_key: bfloat16 [3072, 3072], P(None, 'tile')
- w_value: bfloat16 [3072, 3072], P(None, 'tile'), may hold values from -0.109375 to 0.109375
- q_gain: float32 [3072], P('tile'), as said below
- k_gain: float32 [3072], P('tile'), as said below
- k_cache: bfloat16 [1088, 3072], P('patch', 'tile'), may hold values from -8 to 8
- v_cache: bfloat16 [1088, 3072], P('patch', 'tile'), may hold values from -6 to 6
- w_out: bfloat16 [3072, 3072], P('tile'), may hold values from -0.109375 to 0.109375
- out_gain: float32 [3072], replicated, may hold values from 0.25 to 1.75
- w_final: bfloat16 [3072, 128], replicated, may hold values from -0.109375 to 0.109375
- step_sizes: float32 [2], replicated, may hold values from 0.2 to 0.6
- conv_w: bfloat16 [3, 3, 3, 128, 512], replicated, may hold values from -0.109375 to 0.109375
- conv_b: float32 [512], replicated, may hold values from -3 to 3
Outputs:
- final_latents: float32 [1088, 128], P('patch')
- decoded: bfloat16 [8, 16, 8, 512], P(None, 'patch', 'tile')
The draws below stay inside these ranges and needn't reach their ends.
Inputs may be any that keep to these rules, and one draw needn't show every extreme that they name: `cell_map`: a permutation of the 1024 cells of the grid; entry r is the cell of the r-th video token, which stands in patch shard r // 128; cell (f, h, w) belongs to the decode block (h // 2, w // 2), held by patch index h // 2 and tile index w // 2; every patch shard holds exactly 4 cells of every decode block. A video token's timestamp is 8 times the frame of its cell; audio tokens' timestamps lie in the same span. `q_gain`: positive. `k_gain`: positive.
All inputs are finite; a program needn't handle non-finite values.
Results may differ from the reference program's by a relative error of at most 0.009.
Values may be sent and summed in bfloat16 or wider, within the bound.
A program may use at most 128 MiB of HBM per device.

```python
import jax
import jax.numpy as jnp
from jax import lax

HEADS = 24
HEAD = 128
D = 3072
C = 128
CO = 512
VID_DEV = 128
AUD_DEV = 8
TOK_DEV = 136
TOKENS = 1088
STEPS = 2
FRAMES = 8
BH = 2
BW = 2
HH = 16
WW = 8
CELLS = 32
COUNT = 4
VID_TOTAL = 1024
N_PATCH = 8
N_TILE = 4
DEVICES = 32


def permute_cells(single_key):
    return jax.random.permutation(single_key, CELLS)


def permute_tokens(single_key):
    return jax.random.permutation(single_key, VID_DEV)


def cell_layout(key):
    base_key = jax.random.fold_in(key, 7)
    device_key, shard_key = jax.random.split(base_key)
    local_order = jax.vmap(permute_cells)(jax.random.split(device_key, DEVICES))
    device_ids = jnp.arange(DEVICES, dtype=jnp.int32)[:, None]
    owner_row = device_ids // N_TILE
    owner_column = device_ids % N_TILE
    frame_ids = local_order // (BH * BW)
    inner_row = local_order // BW % BH
    inner_column = local_order % BW
    global_cell = (frame_ids * HH + owner_row * BH + inner_row) * WW + owner_column * BW + inner_column
    by_shard = global_cell.reshape(DEVICES, N_PATCH, COUNT).transpose(1, 0, 2).reshape(N_PATCH, VID_DEV)
    shard_order = jax.vmap(permute_tokens)(jax.random.split(shard_key, N_PATCH))
    shuffled = jnp.take_along_axis(by_shard, shard_order, axis=1)
    return shuffled.reshape(-1).astype(jnp.int32)


def draw_cell_map(key, part):
    return cell_layout(key)


def draw_timestamps(key, part):
    cell_list = cell_layout(key)
    video_times = (cell_list // (HH * WW)).reshape(N_PATCH, VID_DEV) * 8
    audio_times = jax.random.randint(jax.random.fold_in(key, 13), (N_PATCH, AUD_DEV), 0, 8 * FRAMES - 7)
    return jnp.concatenate([video_times, audio_times], axis=1).reshape(-1).astype(jnp.int32)


def paired_weights(key):
    left_matrix = jax.random.normal(jax.random.fold_in(key, 41), (D, D), jnp.float32) * D ** (-0.5)
    right_matrix = jax.random.normal(jax.random.fold_in(key, 43), (D, D), jnp.float32) * D ** (-0.5)
    return (left_matrix, right_matrix)


def draw_w_query(key, part):
    return paired_weights(key)[0].astype(jnp.bfloat16)


def draw_w_key(key, part):
    return paired_weights(key)[1].astype(jnp.bfloat16)


def paired_gain(key, salt):
    spread = jnp.exp(jax.random.uniform(jax.random.fold_in(key, salt), (D,), jnp.float32, 0.0, 0.9163))
    return spread


def draw_q_gain(key, part):
    return paired_gain(key, 61)


def draw_k_gain(key, part):
    return paired_gain(key, 67)


def draw_latents(key, part):
    values = jax.random.normal(jax.random.fold_in(key, 51), (TOKENS, C), jnp.float32)
    return jnp.clip(values, -8.0, 8.0)


def shard_levels(rng, shape, cuts, least, top_value):
    level = 1.0
    for dim, blocks in cuts:
        steps = jax.random.uniform(jax.random.fold_in(jax.random.fold_in(rng, 6), dim), (blocks,), jnp.float32, least / len(cuts), top_value / len(cuts))
        level = level * jnp.repeat(jnp.exp(steps), shape[dim] // blocks).reshape((-1,) + (1,) * (len(shape) - 1 - dim))
    return level


def centred(own_key, extent, deviation, most, cuts=(), kind=jnp.bfloat16):
    drawn = deviation * jax.random.normal(own_key, extent, jnp.float32)
    if cuts:
        drawn = drawn * shard_levels(own_key, extent, cuts, -0.22, 0.18)
    return jnp.clip(drawn, -most, most).astype(kind)


def setup_inputs(seed: int = 0) -> dict:
    key_list = jax.random.split(jax.random.key(seed), 21)
    latents = draw_latents(jax.random.fold_in(key_list[20], 71), 0)
    timestamps = draw_timestamps(jax.random.fold_in(key_list[20], 71), 0)
    cell_map = draw_cell_map(jax.random.fold_in(key_list[20], 71), 0)
    w_video = centred(key_list[3], (C, D), C ** -0.5, 0.5)
    w_audio = centred(key_list[4], (C, D), C ** -0.5, 0.5)
    mod_scale = centred(key_list[5], (STEPS, D), 0.5, 3.0, (), jnp.float32)
    mod_shift = centred(key_list[6], (STEPS, D), 0.5, 3.0, (), jnp.float32)
    w_query = draw_w_query(jax.random.fold_in(key_list[20], 71), 0)
    w_key = draw_w_key(jax.random.fold_in(key_list[20], 71), 0)
    w_value = centred(key_list[9], (D, D), D ** -0.5, 0.109375, ((1, 4),))
    q_gain = draw_q_gain(jax.random.fold_in(key_list[20], 71), 0)
    k_gain = draw_k_gain(jax.random.fold_in(key_list[20], 71), 0)
    k_cache = centred(key_list[12], (TOKENS, D), 1.5, 8.0, ((0, 8), (1, 4)))
    v_cache = centred(key_list[13], (TOKENS, D), 1.0, 6.0, ((0, 8), (1, 4)))
    w_out = centred(key_list[14], (D, D), D ** -0.5, 0.109375, ((0, 4),))
    out_gain = jnp.clip(1.0 + 0.15 * jax.random.normal(key_list[15], (D,), jnp.float32), 0.25, 1.75)
    w_final = centred(key_list[16], (D, C), D ** -0.5, 0.109375)
    step_sizes = jnp.clip(jax.random.uniform(key_list[17], (STEPS,), jnp.float32, 0.2, 0.6), 0.2, 0.6)
    conv_w = centred(key_list[18], (3, 3, 3, C, CO), (27 * C) ** -0.5, 0.109375)
    conv_b = centred(key_list[19], (CO,), 0.5, 3.0, (), jnp.float32)
    return dict(latents=latents, timestamps=timestamps, cell_map=cell_map, w_video=w_video, w_audio=w_audio, mod_scale=mod_scale, mod_shift=mod_shift, w_query=w_query, w_key=w_key, w_value=w_value, q_gain=q_gain, k_gain=k_gain, k_cache=k_cache, v_cache=v_cache, w_out=w_out, out_gain=out_gain, w_final=w_final, step_sizes=step_sizes, conv_w=conv_w, conv_b=conv_b)


EPSILON = 1e-06

def row_scaled(matrix):
    return matrix * lax.rsqrt(lax.optimization_barrier(jnp.mean(matrix * matrix, axis=-1, keepdims=True)) + EPSILON)

def rotate(matrix, stamps):
    half_size = matrix.shape[-1] // 2
    frequency = jnp.exp(-jnp.log(10000.0) * jnp.arange(half_size, dtype=jnp.float32) / half_size)
    angles = stamps.astype(jnp.float32)[:, None, None] * frequency
    cosine = jnp.cos(angles)
    sines = jnp.sin(angles)
    leading = matrix[..., :half_size]
    trailing = matrix[..., half_size:]
    return jnp.concatenate([leading * cosine - trailing * sines, leading * sines + trailing * cosine], axis=-1)

def head_project(normed, weight, gain, stamps):
    raw_out = jnp.dot(normed, weight, preferred_element_type=jnp.float32)
    shaped = raw_out.reshape(raw_out.shape[0], HEADS, HEAD)
    scaled = row_scaled(shaped) * gain.reshape(HEADS, HEAD)
    return rotate(scaled, stamps).reshape(raw_out.shape[0], -1).astype(jnp.bfloat16)

def reference(latents, timestamps, cell_map, w_video, w_audio, mod_scale, mod_shift, w_query, w_key, w_value, q_gain, k_gain, k_cache, v_cache, w_out, out_gain, w_final, step_sizes, conv_w, conv_b):
    shard_of = jnp.arange(TOKENS, dtype=jnp.int32) // TOK_DEV
    same_shard = shard_of[:, None] == shard_of[None, :]
    latent_state = latents
    stale_keys = k_cache
    stale_values = v_cache
    scale_factor = HEAD ** (-0.5)
    for step_index in range(STEPS):
        latent_b = latent_state.astype(jnp.bfloat16).reshape(N_PATCH, TOK_DEV, C)
        video_part = jnp.dot(latent_b[:, :VID_DEV].reshape(-1, C), w_video, preferred_element_type=jnp.float32)
        audio_part = jnp.dot(latent_b[:, VID_DEV:].reshape(-1, C), w_audio, preferred_element_type=jnp.float32)
        embedded = jnp.concatenate([video_part.reshape(N_PATCH, VID_DEV, D), audio_part.reshape(N_PATCH, AUD_DEV, D)], axis=1).reshape(TOKENS, D)
        normed = (row_scaled(embedded) * (1.0 + mod_scale[step_index]) + mod_shift[step_index]).astype(jnp.bfloat16)
        queries = head_project(normed, w_query, q_gain, timestamps)
        fresh_keys = head_project(normed, w_key, k_gain, timestamps)
        values = jnp.dot(normed, w_value, preferred_element_type=jnp.float32).astype(jnp.bfloat16)
        old_keys = stale_keys
        old_values = stale_values

        def one_head(head_index):

            def head_slice(matrix):
                return lax.dynamic_slice_in_dim(matrix, head_index * HEAD, HEAD, 1)
            query_head = head_slice(queries)
            fresh_scores = jnp.dot(query_head, head_slice(fresh_keys).T, preferred_element_type=jnp.float32) * scale_factor
            stale_scores = jnp.dot(query_head, head_slice(old_keys).T, preferred_element_type=jnp.float32) * scale_factor
            scores = jnp.where(same_shard, fresh_scores, stale_scores)
            row_top = lax.optimization_barrier(jnp.max(scores, axis=1, keepdims=True))
            weights = jnp.exp(scores - row_top)
            totals = lax.optimization_barrier(jnp.sum(weights, axis=1, keepdims=True))
            rounded = weights.astype(jnp.bfloat16)
            zero_probs = jnp.zeros_like(rounded)
            result = jnp.dot(jnp.where(same_shard, rounded, zero_probs), head_slice(values), preferred_element_type=jnp.float32)
            result = result + jnp.dot(jnp.where(same_shard, zero_probs, rounded), head_slice(old_values), preferred_element_type=jnp.float32)
            return (result / totals).astype(jnp.bfloat16)
        attended = lax.map(one_head, jnp.arange(HEADS, dtype=jnp.int32))
        attended = attended.transpose(1, 0, 2).reshape(TOKENS, D)
        mixed_rows = embedded + jnp.dot(attended, w_out, preferred_element_type=jnp.float32)
        final_normed = (row_scaled(mixed_rows) * out_gain).astype(jnp.bfloat16)
        velocity = jnp.dot(final_normed, w_final, preferred_element_type=jnp.float32)
        latent_state = latent_state - step_sizes[step_index] * velocity
        stale_keys = fresh_keys
        stale_values = values
    video_rows = latent_state.reshape(N_PATCH, TOK_DEV, C)[:, :VID_DEV].reshape(-1, C).astype(jnp.bfloat16)
    latent_grid = jnp.zeros((VID_TOTAL, C), jnp.bfloat16).at[cell_map].set(video_rows).reshape(FRAMES, HH, WW, C)
    padded = jnp.pad(latent_grid, ((1, 1), (1, 1), (1, 1), (0, 0)))
    columns = jnp.concatenate([padded[shift_time:shift_time + FRAMES, shift_row:shift_row + HH, shift_column:shift_column + WW] for shift_time in range(3) for shift_row in range(3) for shift_column in range(3)], axis=-1)
    conv_out = jnp.dot(columns.reshape(VID_TOTAL, 27 * C), conv_w.reshape(27 * C, CO), preferred_element_type=jnp.float32) + conv_b
    decoded = conv_out.astype(jnp.bfloat16).reshape(FRAMES, HH, WW, CO)
    return (latent_state, decoded)
```

```python
import functools

import jax
import jax.numpy as jnp
from jax import lax
from jax.experimental import pallas as pl
from jax.experimental.pallas import tpu as pltpu
from jax.sharding import PartitionSpec as P

HEAD = 128
VID_DEV = 128
STEPS = 2
FRAMES = 8
BH = 2
EPSILON = 1e-06
MESH = pl.DeviceIdType.MESH
F32 = jnp.float32
BF16 = jnp.bfloat16


def dot(a, b):
    return jnp.dot(a, b, preferred_element_type=F32)


def kernel(
    n,
    nt,
    latents,
    stamps,
    cells,
    mod_scale,
    mod_shift,
    q_gain,
    k_gain,
    k_cache,
    v_cache,
    out_gain,
    step_sizes,
    conv_b,
    wv_hbm,
    wa_hbm,
    wq_hbm,
    wk_hbm,
    wval_hbm,
    wo_hbm,
    wf_hbm,
    cw_hbm,
    state_out,
    conv_out,
    w_vid,
    w_aud,
    w_q,
    w_k,
    w_val,
    w_o,
    w_f,
    kv,
    emb,
    normed,
    q_ref,
    att,
    cos_ref,
    sin_ref,
    acc,
    s1_send,
    s1_recv,
    s2_send,
    s2_recv,
    vel_send,
    vel_recv,
    vid,
    onehot,
    grown,
    load_sem,
    ring_send,
    ring_recv,
    s1_ss,
    s1_rs,
    s2_ss,
    s2_rs,
    v_ss,
    v_rs,
    vid_ss,
    vid_rs,
):
    rows = latents.shape[0]
    pad = kv.shape[4]
    width = emb.shape[1]
    cols = q_ref.shape[1]
    half = cols // 2
    quarter = width // nt
    me = lax.axis_index("patch")
    tile = lax.axis_index("tile")
    core = tile % 2
    ty = tile // 2
    ny = nt // 2

    loads = []
    for i, (src, dst) in enumerate(
        (
            (wv_hbm, w_vid),
            (wa_hbm, w_aud),
            (wk_hbm, w_k),
            (wval_hbm, w_val),
            (wq_hbm, w_q),
            (wo_hbm, w_o),
            (wf_hbm, w_f),
        )
    ):
        copy = pltpu.make_async_copy(src, dst, load_sem.at[i])
        copy.start()
        loads.append(copy)

    barrier = pltpu.get_barrier_semaphore()
    for j in range(1, n):
        pl.semaphore_signal(
            barrier, inc=1, device_id=(lax.rem(me + j, n), tile), device_id_type=MESH
        )
    for j in range(1, nt):
        pl.semaphore_signal(
            barrier, inc=1, device_id=(me, lax.rem(tile + j, nt)), device_id_type=MESH
        )

    for d in range(2):
        for w, src in enumerate((k_cache, v_cache)):
            block = src[:, d * half : (d + 1) * half].astype(F32)
            block = jnp.concatenate([block, jnp.zeros((pad - rows, half), F32)], axis=0)
            kv[1, d, 0, w] = block.astype(BF16)
    pl.semaphore_wait(barrier, n - 1 + nt - 1)

    odd = me % 2
    pos = (1 - odd) * (me // 2) + odd * (n - 1 - me // 2)

    def at_pos(p):
        p = lax.rem(p + n, n)
        back = p // (n // 2)
        return (1 - back) * (2 * p) + back * (2 * (n - 1 - p) + 1)

    nexts = (at_pos(pos + 1), at_pos(pos - 1))

    def hop(step, s, d):
        if s > 0:
            src = kv.at[step, d, s]
        elif step == 0:
            src = kv.at[1, d, 0]
        else:
            src = kv.at[step - 1, d, 0]
        return pltpu.make_async_remote_copy(
            src_ref=src,
            dst_ref=kv.at[step, d, s + 1],
            send_sem=ring_send.at[step, d, s],
            recv_sem=ring_recv.at[step, d, s],
            device_id=(nexts[d], tile),
            device_id_type=MESH,
        )

    queue = [(step, s) for step in range(STEPS) for s in range(n - 1)]
    done = [0]

    def start_hop(index):
        for d in range(2):
            hop(*queue[index], d).start()

    def service(limit=None):
        i = done[0]
        if i >= len(queue) or (limit is not None and queue[i][0] > limit):
            return
        for d in range(2):
            hop(*queue[i], d).wait_recv()
            if i + 1 < len(queue):
                hop(*queue[i + 1], d).start()
        done[0] = i + 1

    start_hop(0)

    lane = lax.broadcasted_iota(jnp.int32, (1, HEAD), 1)
    frequency = jnp.exp(-jnp.log(F32(10000.0)) * (lane % (HEAD // 2)).astype(F32) / (HEAD // 2))
    angles = stamps[...].astype(F32) * frequency
    cos_ref[...] = jnp.cos(angles)
    sin_ref[...] = jnp.where(lane < HEAD // 2, -1.0, 1.0) * jnp.sin(angles)

    bw = VID_DEV // (nt * FRAMES * BH)
    gw = bw + 2
    slots = 2 * FRAMES
    row = lax.broadcasted_iota(jnp.int32, (onehot.shape[0], 1), 0)
    f_id = row % slots - 1
    h_id = row // (slots * gw) - 1 + me * BH
    w_id = row // slots % gw - 1 + tile * bw
    inside = (
        (f_id >= 0)
        & (f_id < FRAMES)
        & (h_id >= 0)
        & (h_id < n * BH)
        & (w_id >= 0)
        & (w_id < nt * bw)
    )
    wanted = jnp.where(inside, (f_id * (n * BH) + h_id) * (nt * bw) + w_id, -1)
    for j in range(n):
        c = slice(j * VID_DEV, (j + 1) * VID_DEV)
        onehot[:, c] = jnp.where(cells[:, c] == wanted, 1.0, 0.0).astype(BF16)

    state_out[...] = latents[...]
    waited = set()

    def need(i):
        if i not in waited:
            loads[i].wait()
            waited.add(i)

    chunk = 256

    def project(weight, gain, put):
        @pl.loop(0, cols // chunk)
        def _(i):
            cs = pl.ds(pl.multiple_of(i * chunk, chunk), chunk)
            raw = dot(normed[...], weight[:, cs])
            for h in range(chunk // HEAD):
                hs = pl.ds(pl.multiple_of(i * chunk + h * HEAD, HEAD), HEAD)
                x = raw[:, h * HEAD : (h + 1) * HEAD]
                if gain is not None:
                    x = x * lax.rsqrt(jnp.mean(x * x, axis=1, keepdims=True) + EPSILON)
                    x = x * gain[:, hs]
                    x = x * cos_ref[...] + pltpu.roll(x, HEAD // 2, 1) * sin_ref[...]
                put(i * (chunk // HEAD) + h, hs, x)

    heads_half = half // HEAD

    for step in range(STEPS):
        need(0)
        need(1)
        state = state_out[...]
        vid_b = state[:VID_DEV].astype(BF16)
        aud_b = state[VID_DEV:].astype(BF16)
        square = jnp.zeros((rows, 1), F32)
        wide = width // 4
        for i in range(4):
            c = slice(i * wide, (i + 1) * wide)
            e = jnp.concatenate([dot(vid_b, w_vid[:, c]), dot(aud_b, w_aud[:, c])], axis=0)
            emb[:, c] = e
            square = square + jnp.sum(e * e, axis=1, keepdims=True)
        scale = lax.rsqrt(square / width + EPSILON)
        for i in range(4):
            c = slice(i * wide, (i + 1) * wide)
            x = emb[:, c] * scale * (1.0 + mod_scale[step : step + 1, c])
            normed[:, c] = (x + mod_shift[step : step + 1, c]).astype(BF16)
        service()

        def put_kv(which):
            def put(h, hs, x):
                x = jnp.concatenate([x, jnp.zeros((pad - rows, HEAD), F32)], axis=0)
                d = h // heads_half
                cs = pl.ds(pl.multiple_of((h % heads_half) * HEAD, HEAD), HEAD)
                kv[step, d, 0, which, :, cs] = x.astype(BF16)

            return put

        def put_q(h, hs, x):
            q_ref[:, hs] = x.astype(BF16)

        need(2)
        if step == 1:
            for d in range(2):
                hop(0, 0, d).wait_send()
        project(w_k, k_gain, put_kv(0))
        service()
        need(3)
        project(w_val, None, put_kv(1))
        service()
        need(4)
        project(w_q, q_gain, put_q)
        if step == STEPS - 1:
            taps = cw_hbm.shape[0]
            out_ch = cw_hbm.shape[1]
            conv_loads = [
                pltpu.make_async_copy(
                    cw_hbm.at[0:width], w_q.at[:, 0:out_ch], load_sem.at[7]
                ),
                pltpu.make_async_copy(
                    cw_hbm.at[width:taps], w_k.at[0 : taps - width, 0:out_ch], load_sem.at[8]
                ),
            ]
            for copy in conv_loads:
                copy.start()
        while done[0] < (step + 1) * (n - 1):
            service()

        for d in range(2):

            @pl.loop(0, heads_half)
            def _(h, d=d):
                hs = pl.ds(pl.multiple_of(h * HEAD, HEAD), HEAD)
                qs = pl.ds(pl.multiple_of(d * half + h * HEAD, HEAD), HEAD)
                keys = kv[step, d, :, 0, :, hs].reshape(n * pad, HEAD)
                values = kv[step, d, :, 1, :, hs].reshape(n * pad, HEAD)
                scores = lax.dot_general(
                    q_ref[:, qs], keys, (((1,), (1,)), ((), ())), preferred_element_type=F32
                )
                key_id = lax.broadcasted_iota(jnp.int32, (1, n * pad), 1)
                scores = jnp.where(key_id % pad < rows, scores, -jnp.inf)
                top = jnp.max(scores, axis=1, keepdims=True)
                weights = jnp.exp((scores - top) * HEAD ** (-0.5))
                total = jnp.sum(weights, axis=1, keepdims=True)
                att[:, qs] = (dot(weights.astype(BF16), values) / total).astype(BF16)

            service()

        need(5)

        def out_part(owner):
            cs = pl.ds(pl.multiple_of(owner * quarter, HEAD), quarter)
            return dot(att[...], w_o[:, cs])

        def pad_rows(x):
            return jnp.concatenate([x, jnp.zeros((pad - rows, x.shape[1]), F32)], axis=0)

        def tile_copy(src, dst, ss, rs, target):
            return pltpu.make_async_remote_copy(
                src_ref=src,
                dst_ref=dst,
                send_sem=ss,
                recv_sem=rs,
                device_id=(me, target),
                device_id_type=MESH,
            )

        sibling = ty * 2 + 1 - core
        first = []
        for j in list(range(1, ny)) + [0]:
            chip = lax.rem(ty + j, ny)
            s1_send[j] = pad_rows(out_part(chip * 2 + 1 - core)).astype(BF16)
            copy = tile_copy(
                s1_send.at[j], s1_recv.at[j], s1_ss.at[step, j], s1_rs.at[step, j], sibling
            )
            copy.start()
            first.append((j, copy))
        second = []
        for j, copy in first:
            chip = lax.rem(ty + j, ny)
            mine = out_part(chip * 2 + core)
            copy.wait_recv()
            mine = mine + s1_recv[j].astype(F32)[:rows]
            if j > 0:
                s2_send[j - 1] = pad_rows(mine).astype(BF16)
                far = tile_copy(
                    s2_send.at[j - 1],
                    s2_recv.at[j - 1],
                    s2_ss.at[step, j],
                    s2_rs.at[step, j],
                    chip * 2 + core,
                )
                far.start()
                second.append((j, far))
            else:
                es = pl.ds(pl.multiple_of(tile * quarter, HEAD), quarter)
                acc[...] = mine + emb[:, es]
        service()
        for j, far in second:
            far.wait_recv()
            acc[...] += s2_recv[j - 1].astype(F32)[:rows]
        need(6)
        mixed = acc[...]
        es = pl.ds(pl.multiple_of(tile * quarter, HEAD), quarter)
        square = jnp.sum(mixed * mixed, axis=1, keepdims=True)
        part = dot((mixed * out_gain[:, es]).astype(BF16), w_f[es, :])
        vel_send[0] = jnp.concatenate(
            [part, jnp.broadcast_to(square, (rows, HEAD))], axis=1
        )
        near = tile_copy(
            vel_send.at[0], vel_recv.at[0], v_ss.at[step, 0], v_rs.at[step, 0], sibling
        )
        near.start()
        near.wait_recv()
        both = vel_send[0] + vel_recv[0]
        vel_send[1] = both
        others = []
        for j in range(1, ny):
            copy = tile_copy(
                vel_send.at[1],
                vel_recv.at[j],
                v_ss.at[step, j],
                v_rs.at[step, j],
                lax.rem(ty + j, ny) * 2 + core,
            )
            copy.start()
            others.append(copy)
        service()
        for j, copy in enumerate(others):
            copy.wait_recv()
            both = both + vel_recv[j + 1]
        channels = part.shape[1]
        scale = lax.rsqrt(both[:, channels : channels + 1] / width + EPSILON)
        state_out[...] = state - step_sizes[step] * (both[:, :channels] * scale)
        for _, copy in first:
            copy.wait_send()
        for _, copy in second:
            copy.wait_send()
        near.wait_send()
        for copy in others:
            copy.wait_send()

    vid[me] = state_out[:VID_DEV, :].astype(BF16)
    sends = []
    for j in list(range(1, n)):
        copy = pltpu.make_async_remote_copy(
            src_ref=vid.at[me],
            dst_ref=vid.at[me],
            send_sem=vid_ss.at[j],
            recv_sem=vid_rs.at[j],
            device_id=(lax.rem(me + j, n), tile),
            device_id_type=MESH,
        )
        copy.start()
        sends.append(copy)
    for index in range(1, len(queue)):
        for d in range(2):
            hop(*queue[index], d).wait_send()
    for copy in conv_loads:
        copy.wait()
    for j in range(1, n):
        source = lax.rem(me - j + n, n)
        pltpu.make_async_remote_copy(
            src_ref=vid.at[source],
            dst_ref=vid.at[source],
            send_sem=vid_ss.at[j],
            recv_sem=vid_rs.at[j],
            device_id=(source, tile),
            device_id_type=MESH,
        ).wait_recv()
    grown[...] = dot(onehot[...], vid[...].reshape(n * VID_DEV, HEAD))
    pieces = []
    for a in range(3):
        for b in range(3):
            for c in range(3):
                starts = [
                    ((h + b) * gw + w + c) * slots + a for h in range(BH) for w in range(bw)
                ]
                pieces.append(
                    jnp.concatenate([grown[s : s + FRAMES, :] for s in starts], axis=0).astype(BF16)
                )
    cut = width // HEAD
    total = dot(jnp.concatenate(pieces[:cut], axis=1), w_q[:, 0:out_ch])
    total = total + dot(jnp.concatenate(pieces[cut:], axis=1), w_k[0 : taps - width, 0:out_ch])
    conv_out[...] = (total + conv_b[...]).astype(BF16)
    for copy in sends:
        copy.wait_send()


def local(
    latents,
    timestamps,
    cell_map,
    w_video,
    w_audio,
    mod_scale,
    mod_shift,
    w_query,
    w_key,
    w_value,
    q_gain,
    k_gain,
    k_cache,
    v_cache,
    w_out,
    out_gain,
    w_final,
    step_sizes,
    conv_w,
    conv_b,
):
    n, nt = lax.axis_size("patch"), lax.axis_size("tile")
    rows, channels = latents.shape
    width = w_query.shape[0]
    cols = w_query.shape[1]
    pad = -(-rows // 16) * 16
    quarter = width // nt
    ny = nt // 2
    bw = VID_DEV // (nt * FRAMES * BH)
    border = (BH + 2) * (bw + 2) * 2 * FRAMES
    cells = FRAMES * BH * bw
    out_ch = conv_w.shape[-1]
    conv_flat = conv_w.reshape(-1, out_ch)
    vmem = pl.BlockSpec(memory_space=pltpu.VMEM)
    hbm = pl.BlockSpec(memory_space=pl.ANY)
    dma = pltpu.SemaphoreType.DMA
    state, conv = pl.pallas_call(
        functools.partial(kernel, n, nt),
        out_shape=(
            jax.ShapeDtypeStruct((rows, channels), F32),
            jax.ShapeDtypeStruct((cells, out_ch), BF16),
        ),
        in_specs=[vmem] * 10 + [pl.BlockSpec(memory_space=pltpu.SMEM), vmem] + [hbm] * 8,
        out_specs=(vmem, vmem),
        scratch_shapes=[
            pltpu.VMEM(w_video.shape, BF16),
            pltpu.VMEM(w_audio.shape, BF16),
            pltpu.VMEM(w_query.shape, BF16),
            pltpu.VMEM(w_key.shape, BF16),
            pltpu.VMEM(w_value.shape, BF16),
            pltpu.VMEM(w_out.shape, BF16),
            pltpu.VMEM(w_final.shape, BF16),
            pltpu.VMEM((STEPS, 2, n, 2, pad, cols // 2), BF16),
            pltpu.VMEM((rows, width), F32),
            pltpu.VMEM((rows, width), BF16),
            pltpu.VMEM((rows, cols), BF16),
            pltpu.VMEM((rows, cols), BF16),
            pltpu.VMEM((rows, HEAD), F32),
            pltpu.VMEM((rows, HEAD), F32),
            pltpu.VMEM((rows, quarter), F32),
            pltpu.VMEM((ny, pad, quarter), BF16),
            pltpu.VMEM((ny, pad, quarter), BF16),
            pltpu.VMEM((ny - 1, pad, quarter), BF16),
            pltpu.VMEM((ny - 1, pad, quarter), BF16),
            pltpu.VMEM((2, rows, channels + HEAD), F32),
            pltpu.VMEM((ny, rows, channels + HEAD), F32),
            pltpu.VMEM((n, VID_DEV, channels), BF16),
            pltpu.VMEM((border, n * VID_DEV), BF16),
            pltpu.VMEM((border, channels), F32),
            dma((9,)),
            dma((STEPS, 2, n - 1)),
            dma((STEPS, 2, n - 1)),
            dma((STEPS, ny)),
            dma((STEPS, ny)),
            dma((STEPS, ny)),
            dma((STEPS, ny)),
            dma((STEPS, ny)),
            dma((STEPS, ny)),
            dma((n,)),
            dma((n,)),
        ],
        compiler_params=pltpu.CompilerParams(
            collective_id=0, has_side_effects=True, vmem_limit_bytes=63 * 1024 * 1024
        ),
    )(
        latents,
        timestamps.reshape(-1, 1),
        cell_map.reshape(1, -1),
        mod_scale,
        mod_shift,
        q_gain.reshape(1, -1),
        k_gain.reshape(1, -1),
        k_cache,
        v_cache,
        out_gain.reshape(1, -1),
        step_sizes,
        conv_b.reshape(1, -1),
        w_video,
        w_audio,
        w_query,
        w_key,
        w_value,
        w_out,
        w_final,
        conv_flat,
    )
    decoded = conv.reshape(BH, bw, FRAMES, out_ch).transpose(2, 0, 1, 3)
    return state, decoded


def solution(mesh):
    return jax.shard_map(
        local,
        mesh=mesh,
        in_specs=(
            P("patch", None),
            P("patch"),
            P(),
            P(),
            P(),
            P(),
            P(),
            P(None, "tile"),
            P(None, "tile"),
            P(None, "tile"),
            P("tile"),
            P("tile"),
            P("patch", "tile"),
            P("patch", "tile"),
            P("tile", None),
            P(),
            P(),
            P(),
            P(),
            P(),
        ),
        out_specs=(P("patch", None), P(None, "patch", "tile", None)),
        check_vma=False,
    )
```

```python
import functools

import jax
import jax.numpy as jnp
from jax import lax
from jax.experimental import pallas as pl
from jax.experimental.pallas import tpu as pltpu
from jax.sharding import PartitionSpec as P

HEAD = 128
VID_DEV = 128
STEPS = 2
FRAMES = 8
BH = 2
EPSILON = 1e-06
MESH = pl.DeviceIdType.MESH
F32 = jnp.float32
BF16 = jnp.bfloat16


def dot(a, b):
    return jnp.dot(a, b, preferred_element_type=F32)


def kernel(
    n,
    nt,
    latents,
    stamps,
    cells,
    mod_scale,
    mod_shift,
    q_gain,
    k_gain,
    k_cache,
    v_cache,
    out_gain,
    step_sizes,
    conv_b,
    wv_hbm,
    wa_hbm,
    wq_hbm,
    wk_hbm,
    wval_hbm,
    wo_hbm,
    wf_hbm,
    cw_hbm,
    state_out,
    conv_out,
    w_vid,
    w_aud,
    w_q,
    w_k,
    w_val,
    w_o,
    w_f,
    kv,
    emb,
    normed,
    q_ref,
    att,
    cos_ref,
    sin_ref,
    acc,
    s1_send,
    s1_recv,
    s2_send,
    s2_recv,
    vel_send,
    vel_recv,
    vid,
    onehot,
    grown,
    load_sem,
    ring_send,
    ring_recv,
    s1_ss,
    s1_rs,
    s2_ss,
    s2_rs,
    v_ss,
    v_rs,
    vid_ss,
    vid_rs,
):
    rows = latents.shape[0]
    pad = kv.shape[4]
    width = emb.shape[1]
    cols = q_ref.shape[1]
    half = cols // 2
    quarter = width // nt
    me = lax.axis_index("patch")
    tile = lax.axis_index("tile")
    core = tile % 2
    ty = tile // 2
    ny = nt // 2

    loads = []
    for i, (src, dst) in enumerate(
        (
            (wv_hbm, w_vid),
            (wa_hbm, w_aud),
            (wk_hbm, w_k),
            (wval_hbm, w_val),
            (wq_hbm, w_q),
            (wo_hbm, w_o),
            (wf_hbm, w_f),
        )
    ):
        copy = pltpu.make_async_copy(src, dst, load_sem.at[i])
        copy.start()
        loads.append(copy)

    barrier = pltpu.get_barrier_semaphore()
    for j in range(1, n):
        pl.semaphore_signal(
            barrier, inc=1, device_id=(lax.rem(me + j, n), tile), device_id_type=MESH
        )
    for j in range(1, nt):
        pl.semaphore_signal(
            barrier, inc=1, device_id=(me, lax.rem(tile + j, nt)), device_id_type=MESH
        )

    for d in range(2):
        for w, src in enumerate((k_cache, v_cache)):
            block = src[:, d * half : (d + 1) * half].astype(F32)
            block = jnp.concatenate([block, jnp.zeros((pad - rows, half), F32)], axis=0)
            kv[1, d, 0, w] = block.astype(BF16)
    pl.semaphore_wait(barrier, n - 1 + nt - 1)

    odd = me % 2
    pos = (1 - odd) * (me // 2) + odd * (n - 1 - me // 2)

    def at_pos(p):
        p = lax.rem(p + n, n)
        back = p // (n // 2)
        return (1 - back) * (2 * p) + back * (2 * (n - 1 - p) + 1)

    nexts = (at_pos(pos + 1), at_pos(pos - 1))

    def hop(step, s, w, d):
        if s > 0:
            src = kv.at[step, d, s, w]
        elif step == 0:
            src = kv.at[1, d, 0, w]
        else:
            src = kv.at[step - 1, d, 0, w]
        return pltpu.make_async_remote_copy(
            src_ref=src,
            dst_ref=kv.at[step, d, s + 1, w],
            send_sem=ring_send.at[step, d, s, w],
            recv_sem=ring_recv.at[step, d, s, w],
            device_id=(nexts[d], tile),
            device_id_type=MESH,
        )

    queue = [(step, s, w) for step in range(STEPS) for s in range(n - 1) for w in range(2)]
    done = [0]

    def start_hop(index):
        for d in range(2):
            hop(*queue[index], d).start()

    def service(limit=None):
        i = done[0]
        if i >= len(queue) or (limit is not None and queue[i][0] > limit):
            return
        for d in range(2):
            hop(*queue[i], d).wait_recv()
            if i + 2 < len(queue):
                hop(*queue[i + 2], d).start()
        done[0] = i + 1

    start_hop(0)
    start_hop(1)

    lane = lax.broadcasted_iota(jnp.int32, (1, HEAD), 1)
    frequency = jnp.exp(-jnp.log(F32(10000.0)) * (lane % (HEAD // 2)).astype(F32) / (HEAD // 2))
    here = lax.broadcasted_iota(jnp.int32, (rows, rows), 0)
    there = lax.broadcasted_iota(jnp.int32, (rows, rows), 1)
    times = jnp.where(here == there, stamps[...].astype(F32), 0.0)
    angles = jnp.sum(times, axis=1, keepdims=True) * frequency
    cos_ref[...] = jnp.cos(angles)
    sin_ref[...] = jnp.where(lane < HEAD // 2, -1.0, 1.0) * jnp.sin(angles)

    bw = VID_DEV // (nt * FRAMES * BH)
    gw = bw + 2
    slots = 2 * FRAMES
    row = lax.broadcasted_iota(jnp.int32, (onehot.shape[0], 1), 0)
    f_id = row % slots - 1
    h_id = row // (slots * gw) - 1 + me * BH
    w_id = row // slots % gw - 1 + tile * bw
    inside = (
        (f_id >= 0)
        & (f_id < FRAMES)
        & (h_id >= 0)
        & (h_id < n * BH)
        & (w_id >= 0)
        & (w_id < nt * bw)
    )
    wanted = jnp.where(inside, (f_id * (n * BH) + h_id) * (nt * bw) + w_id, -1)
    for j in range(n):
        c = slice(j * VID_DEV, (j + 1) * VID_DEV)
        onehot[:, c] = jnp.where(cells[:, c] == wanted, 1.0, 0.0).astype(BF16)

    state_out[...] = latents[...]
    waited = set()

    def need(i):
        if i not in waited:
            loads[i].wait()
            waited.add(i)

    chunk = 256

    def project(weight, gain, put):
        @pl.loop(0, cols // chunk)
        def _(i):
            cs = pl.ds(pl.multiple_of(i * chunk, chunk), chunk)
            raw = dot(normed[...], weight[:, cs])
            for h in range(chunk // HEAD):
                hs = pl.ds(pl.multiple_of(i * chunk + h * HEAD, HEAD), HEAD)
                x = raw[:, h * HEAD : (h + 1) * HEAD]
                if gain is not None:
                    x = x * lax.rsqrt(jnp.mean(x * x, axis=1, keepdims=True) + EPSILON)
                    x = x * gain[pl.ds(i * (chunk // HEAD) + h, 1), :]
                    x = x * cos_ref[...] + pltpu.roll(x, HEAD // 2, 1) * sin_ref[...]
                put(i * (chunk // HEAD) + h, hs, x)

    heads_half = half // HEAD

    for step in range(STEPS):
        need(0)
        need(1)
        state = state_out[...]
        vid_b = state[:VID_DEV].astype(BF16)
        aud_b = state[VID_DEV:].astype(BF16)
        square = jnp.zeros((rows, 1), F32)
        wide = width // 4
        for i in range(4):
            c = slice(i * wide, (i + 1) * wide)
            e = jnp.concatenate([dot(vid_b, w_vid[:, c]), dot(aud_b, w_aud[:, c])], axis=0)
            emb[:, c] = e
            square = square + jnp.sum(e * e, axis=1, keepdims=True)
        scale = lax.rsqrt(square / width + EPSILON)
        for i in range(4):
            c = slice(i * wide, (i + 1) * wide)
            x = emb[:, c] * scale * (1.0 + mod_scale[step : step + 1, c])
            normed[:, c] = (x + mod_shift[step : step + 1, c]).astype(BF16)
        service(step)
        service(step)

        def put_kv(which):
            def put(h, hs, x):
                x = jnp.concatenate([x, jnp.zeros((pad - rows, HEAD), F32)], axis=0)
                d = h // heads_half
                cs = pl.ds(pl.multiple_of((h % heads_half) * HEAD, HEAD), HEAD)
                kv[step, d, 0, which, :, cs] = x.astype(BF16)

            return put

        def put_q(h, hs, x):
            q_ref[:, hs] = x.astype(BF16)

        need(2)
        if step == 1:
            for d in range(2):
                for w in range(2):
                    hop(0, 0, w, d).wait_send()
        project(w_k, k_gain, put_kv(0))
        service(step)
        service(step)
        need(3)
        project(w_val, None, put_kv(1))
        service(step)
        service(step)
        need(4)
        project(w_q, q_gain, put_q)
        if step == STEPS - 1:
            taps = cw_hbm.shape[0]
            out_ch = cw_hbm.shape[1]
            conv_loads = [
                pltpu.make_async_copy(
                    cw_hbm.at[0:width], w_q.at[:, 0:out_ch], load_sem.at[7]
                ),
                pltpu.make_async_copy(
                    cw_hbm.at[width:taps], w_k.at[0 : taps - width, 0:out_ch], load_sem.at[8]
                ),
            ]
            for copy in conv_loads:
                copy.start()
        while done[0] < (step + 1) * 2 * (n - 1):
            service()

        for d in range(2):

            for h in range(heads_half):
                hs = slice(h * HEAD, (h + 1) * HEAD)
                qs = slice(d * half + h * HEAD, d * half + (h + 1) * HEAD)
                keys = kv[step, d, :, 0, :, hs].reshape(n * pad, HEAD)
                values = kv[step, d, :, 1, :, hs].reshape(n * pad, HEAD)
                scores = lax.dot_general(
                    q_ref[:, qs], keys, (((1,), (1,)), ((), ())), preferred_element_type=F32
                )
                key_id = lax.broadcasted_iota(jnp.int32, (1, n * pad), 1)
                scores = jnp.where(key_id % pad < rows, scores, -jnp.inf)
                top = jnp.max(scores, axis=1, keepdims=True)
                weights = jnp.exp((scores - top) * HEAD ** (-0.5))
                total = jnp.sum(weights, axis=1, keepdims=True)
                att[:, qs] = (dot(weights.astype(BF16), values) / total).astype(BF16)
                service()

        need(5)

        def out_part(owner):
            cs = pl.ds(pl.multiple_of(owner * quarter, HEAD), quarter)
            return dot(att[...], w_o[:, cs])

        def pad_rows(x):
            return jnp.concatenate([x, jnp.zeros((pad - rows, x.shape[1]), F32)], axis=0)

        def tile_copy(src, dst, ss, rs, target):
            return pltpu.make_async_remote_copy(
                src_ref=src,
                dst_ref=dst,
                send_sem=ss,
                recv_sem=rs,
                device_id=(me, target),
                device_id_type=MESH,
            )

        sibling = ty * 2 + 1 - core
        first = []
        for j in list(range(1, ny)) + [0]:
            chip = lax.rem(ty + j, ny)
            s1_send[j] = pad_rows(out_part(chip * 2 + 1 - core)).astype(BF16)
            copy = tile_copy(
                s1_send.at[j], s1_recv.at[j], s1_ss.at[step, j], s1_rs.at[step, j], sibling
            )
            copy.start()
            first.append((j, copy))
            service()
        second = []
        for j, copy in first:
            chip = lax.rem(ty + j, ny)
            mine = out_part(chip * 2 + core)
            service()
            copy.wait_recv()
            mine = mine + s1_recv[j].astype(F32)[:rows]
            if j > 0:
                s2_send[j - 1] = pad_rows(mine).astype(BF16)
                far = tile_copy(
                    s2_send.at[j - 1],
                    s2_recv.at[j - 1],
                    s2_ss.at[step, j],
                    s2_rs.at[step, j],
                    chip * 2 + core,
                )
                far.start()
                second.append((j, far))
            else:
                es = pl.ds(pl.multiple_of(tile * quarter, HEAD), quarter)
                acc[...] = mine + emb[:, es]
        service()
        for j, far in second:
            far.wait_recv()
            acc[...] += s2_recv[j - 1].astype(F32)[:rows]
        need(6)
        mixed = acc[...]
        es = pl.ds(pl.multiple_of(tile * quarter, HEAD), quarter)
        square = jnp.sum(mixed * mixed, axis=1, keepdims=True)
        part = dot((mixed * out_gain[:, es]).astype(BF16), w_f[es, :])
        vel_send[0] = jnp.concatenate(
            [part, jnp.broadcast_to(square, (rows, HEAD))], axis=1
        )
        near = tile_copy(
            vel_send.at[0], vel_recv.at[0], v_ss.at[step, 0], v_rs.at[step, 0], sibling
        )
        near.start()
        service()
        near.wait_recv()
        both = vel_send[0] + vel_recv[0]
        vel_send[1] = both
        others = []
        for j in range(1, ny):
            copy = tile_copy(
                vel_send.at[1],
                vel_recv.at[j],
                v_ss.at[step, j],
                v_rs.at[step, j],
                lax.rem(ty + j, ny) * 2 + core,
            )
            copy.start()
            others.append(copy)
        service()
        for j, copy in enumerate(others):
            copy.wait_recv()
            both = both + vel_recv[j + 1]
        channels = part.shape[1]
        scale = lax.rsqrt(both[:, channels : channels + 1] / width + EPSILON)
        state_out[...] = state - step_sizes[step] * (both[:, :channels] * scale)
        for _, copy in first:
            copy.wait_send()
        for _, copy in second:
            copy.wait_send()
        near.wait_send()
        for copy in others:
            copy.wait_send()

    vid[me] = state_out[:VID_DEV, :].astype(BF16)
    sends = []
    for j in list(range(1, n)):
        copy = pltpu.make_async_remote_copy(
            src_ref=vid.at[me],
            dst_ref=vid.at[me],
            send_sem=vid_ss.at[j],
            recv_sem=vid_rs.at[j],
            device_id=(lax.rem(me + j, n), tile),
            device_id_type=MESH,
        )
        copy.start()
        sends.append(copy)
    for index in range(2, len(queue)):
        for d in range(2):
            hop(*queue[index], d).wait_send()
    for copy in conv_loads:
        copy.wait()
    for j in range(1, n):
        source = lax.rem(me - j + n, n)
        pltpu.make_async_remote_copy(
            src_ref=vid.at[source],
            dst_ref=vid.at[source],
            send_sem=vid_ss.at[j],
            recv_sem=vid_rs.at[j],
            device_id=(source, tile),
            device_id_type=MESH,
        ).wait_recv()
    grown[...] = dot(onehot[...], vid[...].reshape(n * VID_DEV, HEAD))
    pieces = []
    for a in range(3):
        for b in range(3):
            for c in range(3):
                starts = [
                    ((h + b) * gw + w + c) * slots + a for h in range(BH) for w in range(bw)
                ]
                pieces.append(
                    jnp.concatenate([grown[s : s + FRAMES, :] for s in starts], axis=0).astype(BF16)
                )
    cut = width // HEAD
    total = dot(jnp.concatenate(pieces[:cut], axis=1), w_q[:, 0:out_ch])
    total = total + dot(jnp.concatenate(pieces[cut:], axis=1), w_k[0 : taps - width, 0:out_ch])
    conv_out[...] = (total + conv_b[...]).astype(BF16)
    for copy in sends:
        copy.wait_send()


def local(
    latents,
    timestamps,
    cell_map,
    w_video,
    w_audio,
    mod_scale,
    mod_shift,
    w_query,
    w_key,
    w_value,
    q_gain,
    k_gain,
    k_cache,
    v_cache,
    w_out,
    out_gain,
    w_final,
    step_sizes,
    conv_w,
    conv_b,
):
    n, nt = lax.axis_size("patch"), lax.axis_size("tile")
    rows, channels = latents.shape
    width = w_query.shape[0]
    cols = w_query.shape[1]
    pad = -(-rows // 16) * 16
    quarter = width // nt
    ny = nt // 2
    bw = VID_DEV // (nt * FRAMES * BH)
    border = (BH + 2) * (bw + 2) * 2 * FRAMES
    cells = FRAMES * BH * bw
    out_ch = conv_w.shape[-1]
    conv_flat = conv_w.reshape(-1, out_ch)
    vmem = pl.BlockSpec(memory_space=pltpu.VMEM)
    hbm = pl.BlockSpec(memory_space=pl.ANY)
    dma = pltpu.SemaphoreType.DMA
    state, conv = pl.pallas_call(
        functools.partial(kernel, n, nt),
        out_shape=(
            jax.ShapeDtypeStruct((rows, channels), F32),
            jax.ShapeDtypeStruct((cells, out_ch), BF16),
        ),
        in_specs=[vmem] * 10 + [pl.BlockSpec(memory_space=pltpu.SMEM), vmem] + [hbm] * 8,
        out_specs=(vmem, vmem),
        scratch_shapes=[
            pltpu.VMEM(w_video.shape, BF16),
            pltpu.VMEM(w_audio.shape, BF16),
            pltpu.VMEM(w_query.shape, BF16),
            pltpu.VMEM(w_key.shape, BF16),
            pltpu.VMEM(w_value.shape, BF16),
            pltpu.VMEM(w_out.shape, BF16),
            pltpu.VMEM(w_final.shape, BF16),
            pltpu.VMEM((STEPS, 2, n, 2, pad, cols // 2), BF16),
            pltpu.VMEM((rows, width), F32),
            pltpu.VMEM((rows, width), BF16),
            pltpu.VMEM((rows, cols), BF16),
            pltpu.VMEM((rows, cols), BF16),
            pltpu.VMEM((rows, HEAD), F32),
            pltpu.VMEM((rows, HEAD), F32),
            pltpu.VMEM((rows, quarter), F32),
            pltpu.VMEM((ny, pad, quarter), BF16),
            pltpu.VMEM((ny, pad, quarter), BF16),
            pltpu.VMEM((ny - 1, pad, quarter), BF16),
            pltpu.VMEM((ny - 1, pad, quarter), BF16),
            pltpu.VMEM((2, rows, channels + HEAD), F32),
            pltpu.VMEM((ny, rows, channels + HEAD), F32),
            pltpu.VMEM((n, VID_DEV, channels), BF16),
            pltpu.VMEM((border, n * VID_DEV), BF16),
            pltpu.VMEM((border, channels), F32),
            dma((9,)),
            dma((STEPS, 2, n - 1, 2)),
            dma((STEPS, 2, n - 1, 2)),
            dma((STEPS, ny)),
            dma((STEPS, ny)),
            dma((STEPS, ny)),
            dma((STEPS, ny)),
            dma((STEPS, ny)),
            dma((STEPS, ny)),
            dma((n,)),
            dma((n,)),
        ],
        compiler_params=pltpu.CompilerParams(
            collective_id=0, has_side_effects=True, vmem_limit_bytes=63 * 1024 * 1024
        ),
    )(
        latents,
        timestamps.reshape(1, -1),
        cell_map.reshape(1, -1),
        mod_scale,
        mod_shift,
        q_gain.reshape(-1, HEAD),
        k_gain.reshape(-1, HEAD),
        k_cache,
        v_cache,
        out_gain.reshape(1, -1),
        step_sizes,
        conv_b.reshape(1, -1),
        w_video,
        w_audio,
        w_query,
        w_key,
        w_value,
        w_out,
        w_final,
        conv_flat,
    )
    decoded = conv.reshape(BH, bw, FRAMES, out_ch).transpose(2, 0, 1, 3)
    return state, decoded


def solution(mesh):
    return jax.shard_map(
        local,
        mesh=mesh,
        in_specs=(
            P("patch", None),
            P("patch"),
            P(),
            P(),
            P(),
            P(),
            P(),
            P(None, "tile"),
            P(None, "tile"),
            P(None, "tile"),
            P("tile"),
            P("tile"),
            P("patch", "tile"),
            P("patch", "tile"),
            P("tile", None),
            P(),
            P(),
            P(),
            P(),
            P(),
        ),
        out_specs=(P("patch", None), P(None, "patch", "tile", None)),
        check_vma=False,
    )
```
